32 devices in a mesh: groups: 2 (over x), row: 16 (over z, y, core).
Axes of the slice: x: 2, y: 2, z: 4, core: 2. Of those that a mesh axis runs over, the one named last changes fastest.
Arguments:
- fine: bfloat16 [2048, 128, 128], P(('groups', 'row')), parts along dimension 0, may hold values from -6 to 6
- parent: bfloat16 [32, 256, 512], P(('groups', 'row')), parts along dimension 0, may hold values from -6 to 6
- coverage: int32 [64, 4], P('groups'), parts along dimension 0, may hold values from 0 to 15
- owner_slot: int32 [32], P('groups'), parts along dimension 0, may hold values from 0 to 15, each once
- w_query: bfloat16 [128, 128], replicated, may hold values from -0.5 to 0.5
- w_key: bfloat16 [512, 128], replicated, may hold values from -0.25 to 0.25
- w_value: bfloat16 [512, 128], replicated, may hold values from -0.25 to 0.25
- norm_gain: float32 [128], replicated, may hold values from 0.1 to 1.9
- conv_weight: bfloat16 [4, 3, 3, 128, 128], replicated, may hold values from -0.25 to 0.25
- conv_bias: float32 [4, 128], replicated, may hold values from -3 to 3
Outputs:
- refined: bfloat16 [2048, 128, 128], P(('groups', 'row')), parts along dimension 0
The draws below stay inside these ranges and needn't reach their ends.
There are 2 independent parts, one for each index of `groups`. The reference program is written for one: setup_inputs(seed, part) draws one part's arguments, and reference() takes and returns one part's arrays. A program takes and returns all parts, laid end to end along the dimension named above; an argument that names none is the same for every part. Nothing has to cross between parts.
Inputs may be any that keep to these rules, and one draw needn't show every extreme that they name: `owner_slot`: each slot exactly once.
All inputs are finite; a program needn't handle non-finite values.
Results may differ from the reference program's by a relative error of at most 0.014.
Values may be sent and summed in bfloat16 or wider, within the bound.
A program may use at most 128 MiB of HBM per device.

```python
import jax
import jax.numpy as jnp
from jax import lax

C = 128
PD = 512
KR = 256
TILE = 64
TCOLS = 2
COVER = 4
LAYERS = 4
NENC = 16
TILES = 32
GRID_H = 1024
GRID_W = 128
N_ROW = 16


def with_ends(values, rng, least, top_value):
    dims = values.shape
    place = [jax.random.randint(jax.random.fold_in(rng, axis), (), 0, dims[axis]) for axis in range(len(dims))]
    values = values.at[tuple(place)].set(least)
    longest = dims.index(max(dims))
    place[longest] = (place[longest] + 1) % dims[longest]
    return values.at[tuple(place)].set(top_value)


def shard_levels(stream_key, shape, pieces, low, top_value):
    loudness = 1.0
    for dim, blocks in pieces:
        steps = jax.random.uniform(jax.random.fold_in(jax.random.fold_in(stream_key, 6), dim), (blocks,), jnp.float32, low / len(pieces), top_value / len(pieces))
        loudness = loudness * jnp.repeat(jnp.exp(steps), shape[dim] // blocks).reshape((-1,) + (1,) * (len(shape) - 1 - dim))
    return loudness


def noise(stream_key, dims, spread, limit, cuts=(), kind=jnp.bfloat16):
    loudness = shard_levels(stream_key, dims, cuts, -0.22, 0.18) if cuts else 1.0
    array = jax.random.normal(stream_key, dims, jnp.float32) * spread * loudness
    return jnp.minimum(jnp.maximum(array, -limit), limit).astype(kind)


def setup_inputs(seed: int = 0, part: int = 0) -> dict:
    key_of = jax.random.split(jax.random.key(seed), 11)
    part_splits = jax.random.split(jax.random.fold_in(key_of[10], part), 11)
    return {
        "fine": noise(part_splits[0], (GRID_H, GRID_W, C), 1.0, 6.0, ((0, 16),)),
        "parent": noise(part_splits[1], (NENC, KR, PD), 1.0, 6.0, ((0, 16),)),
        "coverage": with_ends(jax.random.randint(part_splits[2], (TILES, COVER), 0, NENC), jax.random.fold_in(part_splits[2], 1), 0, NENC - 1).astype(jnp.int32),
        "owner_slot": jax.random.permutation(part_splits[3], NENC).astype(jnp.int32),
        "w_query": noise(key_of[4], (C, C), C ** -0.5, 0.5),
        "w_key": noise(key_of[5], (PD, C), PD ** -0.5, 0.25),
        "w_value": noise(key_of[6], (PD, C), PD ** -0.5, 0.25),
        "norm_gain": jnp.clip(1.0 + 0.18 * jax.random.normal(key_of[7], (C,), jnp.float32), 0.1, 1.9),
        "conv_weight": noise(key_of[8], (LAYERS, 3, 3, C, C), (9 * C // 2) ** -0.5, 0.25),
        "conv_bias": noise(key_of[9], (LAYERS, C), 0.5, 3.0, (), jnp.float32),
    }


def reference(fine, parent, coverage, owner_slot, w_query, w_key, w_value, norm_gain, conv_weight, conv_bias):
    enc_keys = jnp.dot(parent, w_key, preferred_element_type=jnp.float32).astype(jnp.bfloat16)
    enc_values = jnp.dot(parent, w_value, preferred_element_type=jnp.float32).astype(jnp.bfloat16)
    queries = jnp.dot(fine, w_query, preferred_element_type=jnp.float32).astype(jnp.bfloat16)
    tiled = queries.reshape(N_ROW, TILE, TCOLS, TILE, C).transpose(0, 2, 1, 3, 4).reshape(TILES, TILE * TILE, C)

    def one_tile(packed):
        tile_q, tile_cov = packed
        slots = owner_slot[tile_cov]
        tile_k = enc_keys[slots].reshape(COVER * KR, C).astype(jnp.float32)
        tile_v = enc_values[slots].reshape(COVER * KR, C)
        scores = jnp.dot(tile_q.astype(jnp.float32), tile_k.T, precision=lax.Precision.HIGHEST) / jnp.sqrt(jnp.float32(C))
        probs = jax.nn.softmax(scores, axis=-1).astype(jnp.bfloat16)
        return jnp.dot(probs, tile_v, preferred_element_type=jnp.float32)
    attended = lax.map(one_tile, (tiled, coverage))
    attended = attended.reshape(N_ROW, TCOLS, TILE, TILE, C).transpose(0, 2, 1, 3, 4).reshape(GRID_H, GRID_W, C)
    meansq = lax.optimization_barrier(jnp.mean(attended * attended, axis=-1, keepdims=True))
    mixed = (fine.astype(jnp.float32) + norm_gain * attended * lax.rsqrt(meansq + 1e-06)).astype(jnp.bfloat16)
    current = mixed
    for layer_idx in range(LAYERS):
        conv_out = lax.conv_general_dilated(current[None], conv_weight[layer_idx], (1, 1), 'SAME', dimension_numbers=('NHWC', 'HWIO', 'NHWC'), preferred_element_type=jnp.float32)[0]
        current = jax.nn.silu(conv_out + conv_bias[layer_idx]).astype(jnp.bfloat16)
    return current
```

```python
import functools

import jax
import jax.numpy as jnp
from jax import lax
from jax.experimental import pallas as pl
from jax.experimental.pallas import tpu as pltpu
from jax.sharding import PartitionSpec as P

SUB = 16
LOG2E = 1.4426950408889634
VMEM_LIMIT = 56 * 1024 * 1024


def attend_kernel(cover_n, eps, slots_ref, fine_ref, *refs):
    kv_refs = refs[:cover_n]
    gain_ref, out_ref, k_scr, v_scr = refs[cover_n:]
    chans = fine_ref.shape[2]
    key_rows = kv_refs[0].shape[1]

    @pl.when(pl.program_id(1) == 0)
    def _():
        v_scr[...] = jnp.ones_like(v_scr)
        for j in range(cover_n):
            rows = slice(j * key_rows, (j + 1) * key_rows)
            k_scr[:, rows] = kv_refs[j][0, :, :chans].T
            v_scr[rows, :chans] = kv_refs[j][0, :, chans:]

    rows, cols = fine_ref.shape[:2]
    cells = fine_ref[...].reshape(rows * cols, chans)
    half = rows * cols // 2
    for part in range(2):
        mine = cells[part * half : (part + 1) * half]
        scores = jnp.dot(mine, k_scr[...], preferred_element_type=jnp.float32)
        top = jnp.max(scores, axis=-1, keepdims=True)
        weights = jnp.exp2(scores - top).astype(jnp.bfloat16)
        summed = jnp.dot(weights, v_scr[...], preferred_element_type=jnp.float32)
        attended = summed[:, :chans] / summed[:, chans:]
        meansq = jnp.mean(attended * attended, axis=-1, keepdims=True)
        mixed = mine.astype(jnp.float32) + gain_ref[...] * attended * lax.rsqrt(meansq + eps)
        out_ref[part * rows // 2 : (part + 1) * rows // 2] = mixed.astype(jnp.bfloat16).reshape(
            rows // 2, cols, chans
        )


def attend(fine, all_kv, slots, gain, tile_cols):
    side, width, chans = fine.shape
    cover_n = slots.shape[0] // tile_cols
    key_rows = all_kv.shape[1]
    rows = 16
    cells = pl.BlockSpec((rows, width // tile_cols, chans), lambda k, i, slots: (i, k, 0))

    def kv_spec(j):
        return pl.BlockSpec(
            (1, key_rows, 2 * chans), lambda k, i, slots: (slots[k * cover_n + j], 0, 0)
        )

    return pl.pallas_call(
        functools.partial(attend_kernel, cover_n, 1e-06),
        grid_spec=pltpu.PrefetchScalarGridSpec(
            num_scalar_prefetch=1,
            grid=(tile_cols, side // rows),
            in_specs=[cells]
            + [kv_spec(j) for j in range(cover_n)]
            + [pl.BlockSpec((1, chans), lambda k, i, slots: (0, 0))],
            out_specs=cells,
            scratch_shapes=[
                pltpu.VMEM((chans, cover_n * key_rows), jnp.bfloat16),
                pltpu.VMEM((cover_n * key_rows, 2 * chans), jnp.bfloat16),
            ],
        ),
        out_shape=jax.ShapeDtypeStruct(fine.shape, jnp.bfloat16),
        compiler_params=pltpu.CompilerParams(vmem_limit_bytes=VMEM_LIMIT),
        name="attend",
    )(slots, fine, *([all_kv] * cover_n), gain.reshape(1, chans))


def edge_columns(first, last):
    lane = lax.broadcasted_iota(jnp.int32, first.shape, first.ndim - 2)
    axis = first.ndim - 2
    west = jnp.where(lane == 0, 0.0, pltpu.roll(last, 1, axis))
    east = jnp.where(lane == SUB - 1, 0.0, pltpu.roll(first, SUB - 1, axis))
    return west, east


def conv_kernel(
    ends_ref, north_ref, mid_ref, south_ref, w_ref, b_ref, out_ref, wide, state_a, state_b, flat
):
    layers, _, _, chans, _ = w_ref.shape
    side, width, _ = mid_ref.shape
    steps = width // SUB
    halo = north_ref.shape[0]
    batch = flat.shape[0] // width

    def put(dst, parity, pair, num, cells):
        west, east = edge_columns(cells[:, 0], cells[:, steps - 1])
        dst[parity, pl.ds(pair, num), 1 : steps + 1] = cells.astype(jnp.bfloat16)
        dst[parity, pl.ds(pair, num), 0] = west.astype(jnp.bfloat16)
        dst[parity, pl.ds(pair, num), steps + 1] = east.astype(jnp.bfloat16)

    def take_rows(src, src_row, pair, num):
        rows = src[pl.ds(src_row, 2 * num)].astype(jnp.float32)
        flat[0 : 2 * num * width] = rows.reshape(2 * num * width, chans)
        for parity in range(2):
            for p in range(num):
                base = (2 * p + parity) * width
                cells = jnp.stack(
                    [flat[pl.ds(base + i, SUB, stride=steps), :] for i in range(steps)]
                )
                put(state_a, parity, pair + p, 1, cells[None])

    take_rows(north_ref, 0, 0, halo // 2)
    take_rows(south_ref, 0, (halo + side) // 2, halo // 2)
    group = batch // 2

    @pl.loop(0, side // batch)
    def _(c):
        take_rows(mid_ref, c * batch, halo // 2 + c * group, group)

    for layer in range(layers):
        for dx in range(3):
            for r in range(4):
                for o in range(2):
                    dy = r - o
                    at = (dx * 4 + r) * chans
                    if 0 <= dy <= 2:
                        block = w_ref[layer, dy, dx] * jnp.bfloat16(0.5)
                    else:
                        block = jnp.zeros((chans, chans), jnp.bfloat16)
                    wide[layer, at : at + chans, o * chans : (o + 1) * chans] = block

    src, dst = state_a, state_b
    for layer in range(layers):
        pairs = (side + 2 * (halo - 1 - layer)) // 2
        trips = -(-pairs // 8)
        size = -(-pairs // trips)
        bias = b_ref[layer] * 0.5
        bias = jnp.concatenate([bias, bias])[None, :]
        last = layer == layers - 1

        def chunk(pair, num, slot):
            lhs = jnp.concatenate(
                [
                    src[parity, pl.ds(pair + off, num), dx : dx + steps].reshape(num * width, chans)
                    for dx in range(3)
                    for off in range(2)
                    for parity in range(2)
                ],
                axis=1,
            )
            h = jnp.dot(lhs, wide[layer], preferred_element_type=jnp.float32) + bias
            h = h + h * jnp.tanh(h)
            for parity in range(2):
                cells = h[:, parity * chans : (parity + 1) * chans].reshape(num, steps, SUB, chans)
                if not last:
                    put(dst, parity, pair, num, cells)
                    continue
                for p in range(num):
                    base = ((slot + p) * 2 + parity) * width
                    for i in range(steps):
                        flat[pl.ds(base + i, SUB, stride=steps), :] = cells[p, i]
                    out_ref[2 * (pair + p) + parity] = flat[base : base + width, :].astype(
                        jnp.bfloat16
                    )

        @pl.loop(0, trips)
        def _(t):
            start = jnp.minimum(t * size, pairs - size)
            first = size // 2
            chunk(start, first, 0)
            chunk(start + first, size - first, first)

        margin = halo - 1 - layer
        if margin:
            zero_row = jnp.zeros((steps + 2, SUB, chans), jnp.bfloat16)
            for end, low in ((0, 0), (1, 2 * pairs - margin)):

                @pl.when(ends_ref[end] != 0)
                def _():
                    for row in range(low, low + margin):
                        dst[row % 2, row // 2] = zero_row

        src, dst = dst, src


def convolve(ends, north, mid, south, conv_weight, conv_bias):
    layers, _, _, chans, _ = conv_weight.shape
    side, width, _ = mid.shape
    halo = north.shape[0]
    steps = width // SUB
    state = pltpu.VMEM(((2, side // 2 + halo, steps + 2, SUB, chans)), jnp.bfloat16)
    vmem = pl.BlockSpec(memory_space=pltpu.VMEM)
    return pl.pallas_call(
        conv_kernel,
        in_specs=[pl.BlockSpec(memory_space=pltpu.SMEM)] + [vmem] * 5,
        out_specs=vmem,
        out_shape=jax.ShapeDtypeStruct(mid.shape, jnp.bfloat16),
        scratch_shapes=[
            pltpu.VMEM((layers, 12 * chans, 2 * chans), jnp.bfloat16),
            state,
            state,
            pltpu.VMEM((16 * width, chans), jnp.float32),
        ],
        compiler_params=pltpu.CompilerParams(vmem_limit_bytes=VMEM_LIMIT),
        name="convolve",
    )(ends, north, mid, south, conv_weight, conv_bias)


def on_device(
    fine, parent, coverage, owner_slot, w_query, w_key, w_value, norm_gain, conv_weight, conv_bias
):
    side, width, chans = fine.shape
    tile_cols = width // side
    layers = conv_weight.shape[0]
    position = lax.axis_index("row")
    count = lax.axis_size("row")
    local_cov = lax.dynamic_slice_in_dim(coverage, position * tile_cols, tile_cols, 0)
    slots = jnp.take(owner_slot, local_cov.reshape(-1), axis=0)
    f32 = jnp.float32
    keys = jnp.dot(parent[0], w_key, preferred_element_type=f32).astype(jnp.bfloat16)
    keys = jnp.einsum("kd,cd->kc", keys, w_query, preferred_element_type=f32)
    keys = (keys * (LOG2E / chans**0.5)).astype(jnp.bfloat16)
    values = jnp.dot(parent[0], w_value, preferred_element_type=f32).astype(jnp.bfloat16)
    all_kv = lax.all_gather(jnp.concatenate([keys, values], axis=1), "row", axis=0)
    mixed = attend(fine, all_kv, slots, norm_gain, tile_cols)
    north = lax.ppermute(mixed[side - layers :], "row", [(i, i + 1) for i in range(count - 1)])
    south = lax.ppermute(mixed[:layers], "row", [(i + 1, i) for i in range(count - 1)])
    ends = jnp.stack([position == 0, position == count - 1]).astype(jnp.int32)
    return convolve(ends, north, mixed, south, conv_weight, conv_bias)


def solution(mesh):
    spread = P(("groups", "row"), None, None)
    placed = (spread, spread, P("groups", None), P("groups")) + (P(),) * 6
    return jax.shard_map(
        on_device, mesh=mesh, in_specs=placed, out_specs=spread, check_vma=False
    )
```

```python
import functools

import jax
import jax.numpy as jnp
from jax import lax
from jax.experimental import pallas as pl
from jax.experimental.pallas import tpu as pltpu
from jax.sharding import PartitionSpec as P

SUB = 16
LOG2E = 1.4426950408889634
VMEM_LIMIT = 56 * 1024 * 1024
MESH = pl.DeviceIdType.MESH


def flip(z, m):
    bit = 1
    while bit <= m:
        if m & bit:
            z = z + bit - 2 * bit * lax.rem(lax.div(z, bit), 2)
        bit *= 2
    return z


def gather_kernel(
    lines,
    fine_ref,
    parent_ref,
    wq_ref,
    wk_ref,
    wv_ref,
    keys_ref,
    values_ref,
    north_ref,
    south_ref,
    own_k,
    own_v,
    local_sem,
    send_sem,
    recv_sem,
    halo_send,
    halo_recv,
):
    me = lax.axis_index("row")
    count = 4 * lines
    core, col, line = lax.rem(me, 2), lax.rem(lax.div(me, 2), 2), lax.div(me, 4)
    side, halo, chans = fine_ref.shape[0], north_ref.shape[0], wq_ref.shape[0]
    others = [flip(line, m) for m in range(lines)]
    sibling = me + 1 - 2 * core
    across = me + 2 - 4 * col
    along = [z * 4 + col * 2 + core for z in others]
    beyond = [z * 4 + (1 - col) * 2 + core for z in others]
    ring_next, ring_prev = lax.rem(me + 1, count), lax.rem(me + count - 1, count)
    outer = lax.rem(me + 2 * core - 1 + count, count)

    barrier = pltpu.get_barrier_semaphore()
    peers = along[1:] + [across, sibling, outer]
    for peer in peers:
        pl.semaphore_signal(barrier, inc=1, device_id={"row": peer}, device_id_type=MESH)

    parent = parent_ref[0]
    f32 = jnp.float32
    keys = jnp.dot(parent, wk_ref[...], preferred_element_type=f32).astype(jnp.bfloat16)
    keys = lax.dot_general(wq_ref[...], keys, (((1,), (1,)), ((), ())), preferred_element_type=f32)
    own_k[...] = (keys * (LOG2E / chans**0.5)).astype(jnp.bfloat16)
    values = jnp.dot(parent, wv_ref[...], preferred_element_type=f32)
    own_v[...] = values.astype(jnp.bfloat16)
    pl.semaphore_wait(barrier, len(peers))

    held = (keys_ref, values_ref)
    sent = []

    def send(kind, block, peer, src=None):
        copy = pltpu.make_async_remote_copy(
            src_ref=held[kind].at[block] if src is None else src,
            dst_ref=held[kind].at[block],
            send_sem=send_sem.at[len(sent)],
            recv_sem=recv_sem.at[kind, block],
            device_id={"row": peer},
            device_id_type=MESH,
        )
        copy.start()
        sent.append(copy)

    def arrived(kind, block):
        pltpu.make_async_remote_copy(
            src_ref=held[kind].at[block],
            dst_ref=held[kind].at[block],
            send_sem=send_sem.at[0],
            recv_sem=recv_sem.at[kind, block],
            device_id={"row": sibling},
            device_id_type=MESH,
        ).wait_recv()

    for kind, own in enumerate((own_k, own_v)):
        for peer in [across] + along[1:] + [sibling]:
            send(kind, me, peer, own)
    local = [
        pltpu.make_async_copy(own, held[kind].at[me], local_sem.at[kind])
        for kind, own in enumerate((own_k, own_v))
    ]
    edges = [
        pltpu.make_async_remote_copy(
            src_ref=fine_ref.at[pl.ds(first, halo)],
            dst_ref=dst,
            send_sem=halo_send.at[i],
            recv_sem=halo_recv.at[i],
            device_id={"row": peer},
            device_id_type=MESH,
        )
        for i, (first, dst, peer) in enumerate(
            ((side - halo, north_ref, ring_next), (0, south_ref, ring_prev))
        )
    ]
    for copy in local + edges:
        copy.start()

    steps = [("beyond", 0)]
    for m in range(1, lines):
        steps += [("along", m), ("beyond", m)]
    if lines > 1:
        steps[0], steps[1] = steps[1], steps[0]
    for where, m in steps:
        for kind in range(2):
            block = along[m] if where == "along" else beyond[m]
            arrived(kind, block)
            if where == "along":
                send(kind, block, across)
            send(kind, block, sibling)
    for m in range(lines):
        for block in (along[m], beyond[m]):
            for kind in range(2):
                arrived(kind, block + 1 - 2 * core)
    for copy in sent:
        copy.wait_send()
    for copy in local + edges:
        copy.wait()


def gather(fine, parent, w_query, w_key, w_value, count, halo):
    _, width, chans = fine.shape
    key_rows = parent.shape[1]
    lines = count // 4
    vmem, anywhere = pl.BlockSpec(memory_space=pltpu.VMEM), pl.BlockSpec(memory_space=pl.ANY)
    bf16 = jnp.bfloat16
    edge = jax.ShapeDtypeStruct((halo, width, chans), bf16)
    dma = pltpu.SemaphoreType.DMA
    return pl.pallas_call(
        functools.partial(gather_kernel, lines),
        in_specs=[anywhere] + [vmem] * 4,
        out_specs=[anywhere] * 4,
        out_shape=[
            jax.ShapeDtypeStruct((count, chans, key_rows), bf16),
            jax.ShapeDtypeStruct((count, key_rows, chans), bf16),
            edge,
            edge,
        ],
        scratch_shapes=[
            pltpu.VMEM((chans, key_rows), bf16),
            pltpu.VMEM((key_rows, chans), bf16),
            dma((2,)),
            dma((2 * (count - 1),)),
            dma((2, count)),
            dma((2,)),
            dma((2,)),
        ],
        compiler_params=pltpu.CompilerParams(collective_id=0, has_side_effects=True),
        name="gather",
    )(fine, parent, w_query, w_key, w_value)


def edge_columns(first, last):
    lane = lax.broadcasted_iota(jnp.int32, first.shape, first.ndim - 2)
    axis = first.ndim - 2
    west = jnp.where(lane == 0, 0.0, pltpu.roll(last, 1, axis))
    east = jnp.where(lane == SUB - 1, 0.0, pltpu.roll(first, SUB - 1, axis))
    return west, east


def step_kernel(
    tile_cols,
    cover_ref,
    owner_ref,
    fine_ref,
    north_ref,
    south_ref,
    keys_ref,
    values_ref,
    gain_ref,
    w_ref,
    b_ref,
    out_ref,
    tile_k,
    tile_v,
    scores_a,
    scores_b,
    mixed,
    wide,
    state_a,
    state_b,
    flat,
):
    layers, _, _, chans, _ = w_ref.shape
    side, width, _ = fine_ref.shape
    steps = width // SUB
    halo = north_ref.shape[0]
    batch = flat.shape[0] // width
    position, count = lax.axis_index("row"), keys_ref.shape[0]
    key_rows = values_ref.shape[1]
    span = width // tile_cols
    rows_at_once = scores_a.shape[0] // span

    def fill(tile_row, k):
        for j in range(cover_ref.shape[1]):
            slot = owner_ref[cover_ref[tile_row * tile_cols + k, j]]
            rows = slice(j * key_rows, (j + 1) * key_rows)
            tile_k[:, rows] = keys_ref[slot]
            tile_v[rows, :chans] = values_ref[slot]

    def cells_of(src, row, k):
        block = src[pl.ds(row, rows_at_once), k * span : (k + 1) * span]
        return block.reshape(rows_at_once * span, chans)

    def score(src, row, k, dst):
        dst[...] = jnp.dot(cells_of(src, row, k), tile_k[...], preferred_element_type=jnp.float32)

    def blend(src, row, k, scores, at):
        top = jnp.max(scores[...], axis=-1, keepdims=True)
        weights = jnp.exp2(scores[...] - top).astype(jnp.bfloat16)
        summed = jnp.dot(weights, tile_v[...], preferred_element_type=jnp.float32)
        attended = summed[:, :chans] / summed[:, chans:]
        meansq = jnp.mean(attended * attended, axis=-1, keepdims=True)
        cells = cells_of(src, row, k).astype(jnp.float32)
        new = cells + gain_ref[...] * attended * lax.rsqrt(meansq + 1e-06)
        mixed[pl.ds(at + row, rows_at_once), k * span : (k + 1) * span] = new.astype(
            jnp.bfloat16
        ).reshape(rows_at_once, span, chans)

    tile_v[...] = jnp.ones_like(tile_v)
    above, below = jnp.maximum(position - 1, 0), jnp.minimum(position + 1, count - 1)
    for src, tile_row, at in ((north_ref, above, 0), (south_ref, below, halo + side)):
        for k in range(tile_cols):
            fill(tile_row, k)
            score(src, 0, k, scores_a)
            blend(src, 0, k, scores_a, at)
    for k in range(tile_cols):
        fill(position, k)
        score(fine_ref, 0, k, scores_a)

        @pl.loop(0, side, step=2 * rows_at_once)
        def _(row):
            middle = row + rows_at_once
            score(fine_ref, middle, k, scores_b)
            blend(fine_ref, row, k, scores_a, halo)
            score(fine_ref, jnp.minimum(middle + rows_at_once, side - rows_at_once), k, scores_a)
            blend(fine_ref, middle, k, scores_b, halo)

    at_end = (position == 0, position == count - 1)
    for end, low in ((0, 0), (1, halo + side)):

        @pl.when(at_end[end])
        def _():
            mixed[low : low + halo] = jnp.zeros((halo, width, chans), jnp.bfloat16)

    def put(dst, parity, pair, num, cells):
        west, east = edge_columns(cells[:, 0], cells[:, steps - 1])
        dst[parity, pl.ds(pair, num), 1 : steps + 1] = cells.astype(jnp.bfloat16)
        dst[parity, pl.ds(pair, num), 0] = west.astype(jnp.bfloat16)
        dst[parity, pl.ds(pair, num), steps + 1] = east.astype(jnp.bfloat16)

    def take_rows(src, src_row, pair, num):
        rows = src[pl.ds(src_row, 2 * num)].astype(jnp.float32)
        flat[0 : 2 * num * width] = rows.reshape(2 * num * width, chans)
        for parity in range(2):
            for p in range(num):
                base = (2 * p + parity) * width
                cells = jnp.stack(
                    [flat[pl.ds(base + i, SUB, stride=steps), :] for i in range(steps)]
                )
                put(state_a, parity, pair + p, 1, cells[None])

    @pl.loop(0, (side + 2 * halo) // 8)
    def _(c):
        take_rows(mixed, c * 8, c * 4, 4)

    for layer in range(layers):
        for dx in range(3):
            for r in range(4):
                for o in range(2):
                    dy = r - o
                    at = (dx * 4 + r) * chans
                    if 0 <= dy <= 2:
                        block = w_ref[layer, dy, dx] * jnp.bfloat16(0.5)
                    else:
                        block = jnp.zeros((chans, chans), jnp.bfloat16)
                    wide[layer, at : at + chans, o * chans : (o + 1) * chans] = block

    src, dst = state_a, state_b
    for layer in range(layers):
        pairs = (side + 2 * (halo - 1 - layer)) // 2
        trips = -(-pairs // 8)
        size = -(-pairs // trips)
        bias = b_ref[layer] * 0.5
        bias = jnp.concatenate([bias, bias])[None, :]
        last = layer == layers - 1

        def chunk(pair, num, slot):
            lhs = jnp.concatenate(
                [
                    src[parity, pl.ds(pair + off, num), dx : dx + steps].reshape(num * width, chans)
                    for dx in range(3)
                    for off in range(2)
                    for parity in range(2)
                ],
                axis=1,
            )
            h = jnp.dot(lhs, wide[layer], preferred_element_type=jnp.float32) + bias
            h = h + h * jnp.tanh(h)
            for parity in range(2):
                cells = h[:, parity * chans : (parity + 1) * chans].reshape(num, steps, SUB, chans)
                if not last:
                    put(dst, parity, pair, num, cells)
                    continue
                for p in range(num):
                    base = ((slot + p) * 2 + parity) * width
                    for i in range(steps):
                        flat[pl.ds(base + i, SUB, stride=steps), :] = cells[p, i]
                    out_ref[2 * (pair + p) + parity] = flat[base : base + width, :].astype(
                        jnp.bfloat16
                    )

        @pl.loop(0, trips)
        def _(t):
            start = jnp.minimum(t * size, pairs - size)
            first = size // 2
            chunk(start, first, 0)
            chunk(start + first, size - first, first)

        margin = halo - 1 - layer
        if margin:
            zero_row = jnp.zeros((steps + 2, SUB, chans), jnp.bfloat16)
            for end, low in ((0, 0), (1, 2 * pairs - margin)):

                @pl.when(at_end[end])
                def _():
                    for row in range(low, low + margin):
                        dst[row % 2, row // 2] = zero_row

        src, dst = dst, src


def step(fine, north, south, all_keys, all_values, coverage, owner_slot, gain, weight, bias):
    layers, _, _, chans, _ = weight.shape
    side, width, _ = fine.shape
    halo = north.shape[0]
    tile_cols = width // side
    keys = coverage.shape[1] * all_values.shape[1]
    at_once = halo * side
    bf16, f32 = jnp.bfloat16, jnp.float32
    state = pltpu.VMEM((2, side // 2 + halo, width // SUB + 2, SUB, chans), bf16)
    vmem, smem = pl.BlockSpec(memory_space=pltpu.VMEM), pl.BlockSpec(memory_space=pltpu.SMEM)
    return pl.pallas_call(
        functools.partial(step_kernel, tile_cols),
        in_specs=[smem] * 2 + [vmem] * 8,
        out_specs=vmem,
        out_shape=jax.ShapeDtypeStruct(fine.shape, bf16),
        scratch_shapes=[
            pltpu.VMEM((chans, keys), bf16),
            pltpu.VMEM((keys, 2 * chans), bf16),
            pltpu.VMEM((at_once, keys), f32),
            pltpu.VMEM((at_once, keys), f32),
            pltpu.VMEM((side + 2 * halo, width, chans), bf16),
            pltpu.VMEM((layers, 12 * chans, 2 * chans), bf16),
            state,
            state,
            pltpu.VMEM((16 * width, chans), f32),
        ],
        compiler_params=pltpu.CompilerParams(vmem_limit_bytes=VMEM_LIMIT),
        name="step",
    )(
        coverage,
        owner_slot,
        fine,
        north,
        south,
        all_keys,
        all_values,
        gain.reshape(1, chans),
        weight,
        bias,
    )


def on_device(
    fine, parent, coverage, owner_slot, w_query, w_key, w_value, norm_gain, conv_weight, conv_bias
):
    count, halo = lax.axis_size("row"), conv_weight.shape[0]
    keys, values, north, south = gather(fine, parent, w_query, w_key, w_value, count, halo)
    return step(
        fine, north, south, keys, values, coverage, owner_slot, norm_gain, conv_weight, conv_bias
    )


def solution(mesh):
    spread = P(("groups", "row"), None, None)
    placed = (spread, spread, P("groups", None), P("groups")) + (P(),) * 6
    return jax.shard_map(
        on_device, mesh=mesh, in_specs=placed, out_specs=spread, check_vma=False
    )
```

```python
import functools

import jax
import jax.numpy as jnp
from jax import lax
from jax.experimental import pallas as pl
from jax.experimental.pallas import tpu as pltpu
from jax.sharding import PartitionSpec as P

SUB = 16
LOG2E = 1.4426950408889634
VMEM_LIMIT = 40 * 1024 * 1024
MESH = pl.DeviceIdType.MESH


def gather_kernel(
    lines,
    fine_ref,
    parent_ref,
    wq_ref,
    wk_ref,
    wv_ref,
    keys_ref,
    values_ref,
    north_ref,
    south_ref,
    own_k,
    own_v,
    local_sem,
    send_sem,
    recv_sem,
    halo_send,
    halo_recv,
):
    me = lax.axis_index("row")
    count = 4 * lines
    core, col, line = lax.rem(me, 2), lax.rem(lax.div(me, 2), 2), lax.div(me, 4)
    side, halo, chans = fine_ref.shape[0], north_ref.shape[0], wq_ref.shape[0]
    sibling = me + 1 - 2 * core
    across = me + 2 - 4 * col
    ring_next, ring_prev = lax.rem(me + 1, count), lax.rem(me + count - 1, count)
    outer = lax.rem(me + 2 * core - 1 + count, count)
    up = (line < lines - 1, me + 4)
    down = (line > 0, me - 4)

    barrier = pltpu.get_barrier_semaphore()
    for peer in (across, sibling, outer):
        pl.semaphore_signal(barrier, inc=1, device_id={"row": peer}, device_id_type=MESH)
    for exists, peer in (up, down):

        @pl.when(exists)
        def _():
            pl.semaphore_signal(barrier, inc=1, device_id={"row": peer}, device_id_type=MESH)

    parent = parent_ref[0]
    f32 = jnp.float32
    keys = jnp.dot(parent, wk_ref[...], preferred_element_type=f32).astype(jnp.bfloat16)
    keys = lax.dot_general(wq_ref[...], keys, (((1,), (1,)), ((), ())), preferred_element_type=f32)
    own_k[...] = (keys * (LOG2E / chans**0.5)).astype(jnp.bfloat16)
    values = jnp.dot(parent, wv_ref[...], preferred_element_type=f32)
    own_v[...] = values.astype(jnp.bfloat16)
    inside = jnp.minimum(line, 1) + jnp.minimum(lines - 1 - line, 1)
    pl.semaphore_wait(barrier, 3 + inside)

    held = (keys_ref, values_ref)
    owned = (own_k, own_v)

    def copy_of(way, kind, block, turn, peer, own=False):
        return pltpu.make_async_remote_copy(
            src_ref=owned[kind] if own else held[kind].at[block],
            dst_ref=held[kind].at[block],
            send_sem=send_sem.at[way, kind, turn],
            recv_sem=recv_sem.at[kind, block],
            device_id={"row": peer},
            device_id_type=MESH,
        )

    def arrived(kind, block):
        copy_of(3, kind, block, 0, sibling).wait_recv()

    for kind in range(2):
        for way, (exists, peer) in enumerate((up, down)):

            @pl.when(exists)
            def _():
                copy_of(way, kind, me, 0, peer, True).start()

        copy_of(2, kind, me, 0, across, True).start()
    for kind in range(2):
        copy_of(3, kind, me, 0, sibling, True).start()
    local = [pltpu.make_async_copy(owned[k], held[k].at[me], local_sem.at[k]) for k in range(2)]
    edges = [
        pltpu.make_async_remote_copy(
            src_ref=fine_ref.at[pl.ds(first, halo)],
            dst_ref=dst,
            send_sem=halo_send.at[i],
            recv_sem=halo_recv.at[i],
            device_id={"row": peer},
            device_id_type=MESH,
        )
        for i, (first, dst, peer) in enumerate(
            ((side - halo, north_ref, ring_next), (0, south_ref, ring_prev))
        )
    ]
    for copy in local:
        copy.start()

    for t in range(lines):
        for kind in range(2):
            if t:
                for way, (exists, peer) in enumerate((up, down)):
                    block = me - 4 * t if way == 0 else me + 4 * t

                    @pl.when(line >= t if way == 0 else line < lines - t)
                    def _():
                        arrived(kind, block)

                        @pl.when(exists)
                        def _():
                            copy_of(way, kind, block, t, peer).start()

                        copy_of(2, kind, block, 2 * t + way, across).start()
                        copy_of(3, kind, block, 4 * t + way, sibling).start()

        for kind in range(2):
            for way in range(2 if t else 1):
                source = across - 4 * t if way == 0 else across + 4 * t

                @pl.when(line >= t if way == 0 else line < lines - t)
                def _():
                    arrived(kind, source)
                    copy_of(3, kind, source, 4 * t + 2 + way, sibling).start()

    for copy in edges:
        copy.start()

    for t in range(lines):
        for way in range(2 if t else 1):
            shift = -4 * t if way == 0 else 4 * t

            @pl.when(line >= t if way == 0 else line < lines - t)
            def _():
                for kind in range(2):
                    arrived(kind, sibling + shift)
                    arrived(kind, sibling + (across - me) + shift)
                    copy_of(2, kind, me, 2 * t + way, across).wait_send()
                    copy_of(3, kind, me, 4 * t + way, sibling).wait_send()
                    copy_of(3, kind, me, 4 * t + 2 + way, sibling).wait_send()

        for way, (exists, peer) in enumerate((up, down)):
            has = line >= t if way == 0 else line < lines - t

            @pl.when(jnp.logical_and(has, exists))
            def _():
                for kind in range(2):
                    copy_of(way, kind, me, t, peer).wait_send()

    for copy in local + edges:
        copy.wait()


def gather(fine, parent, w_query, w_key, w_value, count, halo):
    _, width, chans = fine.shape
    key_rows = parent.shape[1]
    lines = count // 4
    vmem, anywhere = pl.BlockSpec(memory_space=pltpu.VMEM), pl.BlockSpec(memory_space=pl.ANY)
    bf16 = jnp.bfloat16
    edge = jax.ShapeDtypeStruct((halo, width, chans), bf16)
    dma = pltpu.SemaphoreType.DMA
    return pl.pallas_call(
        functools.partial(gather_kernel, lines),
        in_specs=[anywhere] + [vmem] * 4,
        out_specs=[vmem] * 2 + [anywhere] * 2,
        out_shape=[
            jax.ShapeDtypeStruct((count, chans, key_rows), bf16),
            jax.ShapeDtypeStruct((count, key_rows, chans), bf16),
            edge,
            edge,
        ],
        scratch_shapes=[
            pltpu.VMEM((chans, key_rows), bf16),
            pltpu.VMEM((key_rows, chans), bf16),
            dma((2,)),
            dma((4, 2, 4 * lines)),
            dma((2, count)),
            dma((2,)),
            dma((2,)),
        ],
        compiler_params=pltpu.CompilerParams(
            collective_id=0, has_side_effects=True, vmem_limit_bytes=16 * 1024 * 1024
        ),
        name="gather",
    )(fine, parent, w_query, w_key, w_value)


def edge_columns(first, last):
    lane = lax.broadcasted_iota(jnp.int32, first.shape, first.ndim - 2)
    axis = first.ndim - 2
    west = jnp.where(lane == 0, 0.0, pltpu.roll(last, 1, axis))
    east = jnp.where(lane == SUB - 1, 0.0, pltpu.roll(first, SUB - 1, axis))
    return west, east


def step_kernel(
    tile_cols,
    cover_ref,
    owner_ref,
    fine_ref,
    north_ref,
    south_ref,
    keys_ref,
    values_ref,
    gain_ref,
    w_ref,
    b_ref,
    out_ref,
    tile_k,
    tile_v,
    scores_a,
    scores_b,
    weights_a,
    weights_b,
    mixed,
    wide,
    state_a,
    state_b,
    flat,
    acc_a,
    acc_b,
    sems,
):
    layers, _, _, chans, _ = w_ref.shape
    side, width, _ = fine_ref.shape
    steps = width // SUB
    halo = north_ref.shape[0]
    position, count = lax.axis_index("row"), keys_ref.shape[0]
    key_rows = values_ref.shape[1]
    span = width // tile_cols
    cells = halo * span
    blocks = (side + 2 * halo) // halo
    chunks = tile_cols * blocks

    loads = [
        pltpu.make_async_copy(src, mixed.at[pl.ds(at, src.shape[0])], sems.at[i])
        for i, (src, at) in enumerate(
            ((north_ref, 0), (fine_ref, halo), (south_ref, halo + side))
        )
    ]
    for copy in loads:
        copy.start()
    above, below = jnp.maximum(position - 1, 0), jnp.minimum(position + 1, count - 1)
    for k in range(tile_cols):
        for place, tile_row in enumerate((above, position, below)):
            for j in range(cover_ref.shape[1]):
                slot = owner_ref[cover_ref[tile_row * tile_cols + k, j]]
                rows = slice(j * key_rows, (j + 1) * key_rows)
                tile_k[3 * k + place, :, rows] = keys_ref[slot]
                tile_v[3 * k + place, rows, :chans] = values_ref[slot]
                tile_v[3 * k + place, rows, chans:] = jnp.ones((key_rows, chans), jnp.bfloat16)
    for copy in loads:
        copy.wait()

    def place_of(c):
        k, block = lax.div(c, blocks), lax.rem(c, blocks)
        tile = 3 * k + jnp.minimum(block, 1) + jnp.maximum(block - (blocks - 2), 0)
        return tile, pl.ds(block * halo, halo), pl.ds(pl.multiple_of(k * span, span), span)

    def score(c, dst):
        tile, rows, cols = place_of(c)
        mine = mixed[rows, cols].reshape(cells, chans)
        dst[...] = jnp.dot(mine, tile_k[tile], preferred_element_type=jnp.float32)

    def soften(src, dst):
        for at in range(0, cells, 32):
            some = src[at : at + 32]
            top = jnp.max(some, axis=-1, keepdims=True)
            dst[at : at + 32] = jnp.exp2(some - top).astype(jnp.bfloat16)

    def blend(c, weights):
        tile, rows, cols = place_of(c)
        summed = jnp.dot(weights[...], tile_v[tile], preferred_element_type=jnp.float32)
        attended = summed[:, :chans] / summed[:, chans:]
        meansq = jnp.mean(attended * attended, axis=-1, keepdims=True)
        mine = mixed[rows, cols].reshape(cells, chans).astype(jnp.float32)
        new = mine + gain_ref[...] * attended * lax.rsqrt(meansq + 1e-06)
        mixed[rows, cols] = new.astype(jnp.bfloat16).reshape(halo, span, chans)

    score(0, scores_a)
    score(1, scores_b)
    soften(scores_a, weights_a)

    @pl.loop(1, chunks - 1, step=2)
    def _(c):
        score(c + 1, scores_a)
        soften(scores_b, weights_b)
        blend(c - 1, weights_a)
        score(c + 2, scores_b)
        soften(scores_a, weights_a)
        blend(c, weights_b)

    soften(scores_b, weights_b)
    blend(chunks - 2, weights_a)
    blend(chunks - 1, weights_b)

    at_end = (position == 0, position == count - 1)
    for end, low in ((0, 0), (1, halo + side)):

        @pl.when(at_end[end])
        def _():
            mixed[low : low + halo] = jnp.zeros((halo, width, chans), jnp.bfloat16)

    def put(dst, parity, pair, num, cells):
        west, east = edge_columns(cells[:, 0], cells[:, steps - 1])
        dst[parity, pl.ds(pair, num), 1 : steps + 1] = cells.astype(jnp.bfloat16)
        dst[parity, pl.ds(pair, num), 0] = west.astype(jnp.bfloat16)
        dst[parity, pl.ds(pair, num), steps + 1] = east.astype(jnp.bfloat16)

    def take_rows(src, src_row, pair, num):
        rows = src[pl.ds(src_row, 2 * num)].astype(jnp.float32)
        flat[0 : 2 * num * width] = rows.reshape(2 * num * width, chans)
        for parity in range(2):
            for p in range(num):
                base = (2 * p + parity) * width
                cells = jnp.stack(
                    [flat[pl.ds(base + i, SUB, stride=steps), :] for i in range(steps)]
                )
                put(state_a, parity, pair + p, 1, cells[None])

    @pl.loop(0, (side + 2 * halo) // 8)
    def _(c):
        take_rows(mixed, c * 8, c * 4, 4)

    for layer in range(layers):
        for dx in range(3):
            for r in range(4):
                for o in range(2):
                    dy = r - o
                    at = (dx * 4 + r) * chans
                    if 0 <= dy <= 2:
                        block = w_ref[layer, dy, dx] * jnp.bfloat16(0.5)
                    else:
                        block = jnp.zeros((chans, chans), jnp.bfloat16)
                    wide[layer, at : at + chans, o * chans : (o + 1) * chans] = block

    src, dst = state_a, state_b
    for layer in range(layers):
        pairs = (side + 2 * (halo - 1 - layer)) // 2
        last = layer == layers - 1
        size = min((4, 5), key=lambda n: (-(-pairs // n) * n, -n))
        trips = -(-pairs // size)
        bias = b_ref[layer] * 0.5
        bias = jnp.concatenate([bias, bias])[None, :]

        def first_of(t):
            return jnp.minimum(t * size, pairs - size)

        def multiply(t, acc):
            pair = first_of(t)
            lhs = jnp.concatenate(
                [
                    src[parity, pl.ds(pair + off, size), dx : dx + steps].reshape(
                        size * width, chans
                    )
                    for dx in range(3)
                    for off in range(2)
                    for parity in range(2)
                ],
                axis=1,
            )
            acc[: size * width] = jnp.dot(lhs, wide[layer], preferred_element_type=jnp.float32)

        def activate(t, acc, base):
            pair = first_of(t)
            for p in range(size):
                h = acc[p * width : (p + 1) * width] + bias
                h = h + h * jnp.tanh(h)
                for parity in range(2):
                    cells = h[:, parity * chans : (parity + 1) * chans]
                    cells = cells.reshape(1, steps, SUB, chans)
                    if not last:
                        put(dst, parity, pair + p, 1, cells)
                        continue
                    at = base + (2 * p + parity) * width
                    for i in range(steps):
                        flat[pl.ds(at + i, SUB, stride=steps), :] = cells[0, i]
                    out_ref[2 * (pair + p) + parity] = flat[at : at + width, :].astype(
                        jnp.bfloat16
                    )

        multiply(0, acc_a)

        @pl.loop(0, (trips - 1) // 2)
        def _(t):
            multiply(2 * t + 1, acc_b)
            activate(2 * t, acc_a, 0)
            multiply(2 * t + 2, acc_a)
            activate(2 * t + 1, acc_b, 2 * size * width)

        if trips % 2 == 0:
            multiply(trips - 1, acc_b)
            activate(trips - 2, acc_a, 0)
            activate(trips - 1, acc_b, 2 * size * width)
        else:
            activate(trips - 1, acc_a, 0)

        margin = halo - 1 - layer
        if margin:
            zero_row = jnp.zeros((steps + 2, SUB, chans), jnp.bfloat16)
            for end, low in ((0, 0), (1, 2 * pairs - margin)):

                @pl.when(at_end[end])
                def _():
                    for row in range(low, low + margin):
                        dst[row % 2, row // 2] = zero_row

        src, dst = dst, src


def step(fine, north, south, all_keys, all_values, coverage, owner_slot, gain, weight, bias):
    layers, _, _, chans, _ = weight.shape
    side, width, _ = fine.shape
    halo = north.shape[0]
    tile_cols = width // side
    keys = coverage.shape[1] * all_values.shape[1]
    at_once = halo * side
    bf16, f32 = jnp.bfloat16, jnp.float32
    state = pltpu.VMEM((2, side // 2 + halo, width // SUB + 2, SUB, chans), bf16)
    vmem, smem = pl.BlockSpec(memory_space=pltpu.VMEM), pl.BlockSpec(memory_space=pltpu.SMEM)
    return pl.pallas_call(
        functools.partial(step_kernel, tile_cols),
        in_specs=[smem] * 2 + [pl.BlockSpec(memory_space=pl.ANY)] * 3 + [vmem] * 5,
        out_specs=vmem,
        out_shape=jax.ShapeDtypeStruct(fine.shape, bf16),
        scratch_shapes=[
            pltpu.VMEM((3 * tile_cols, chans, keys), bf16),
            pltpu.VMEM((3 * tile_cols, keys, 2 * chans), bf16),
            pltpu.VMEM((at_once, keys), f32),
            pltpu.VMEM((at_once, keys), f32),
            pltpu.VMEM((at_once, keys), bf16),
            pltpu.VMEM((at_once, keys), bf16),
            pltpu.VMEM((side + 2 * halo, width, chans), bf16),
            pltpu.VMEM((layers, 12 * chans, 2 * chans), bf16),
            state,
            state,
            pltpu.VMEM((20 * width, chans), f32),
            pltpu.VMEM((5 * width, 2 * chans), f32),
            pltpu.VMEM((5 * width, 2 * chans), f32),
            pltpu.SemaphoreType.DMA((3,)),
        ],
        compiler_params=pltpu.CompilerParams(vmem_limit_bytes=VMEM_LIMIT),
        name="step",
    )(
        coverage,
        owner_slot,
        fine,
        north,
        south,
        all_keys,
        all_values,
        gain.reshape(1, chans),
        weight,
        bias,
    )


def on_device(
    fine, parent, coverage, owner_slot, w_query, w_key, w_value, norm_gain, conv_weight, conv_bias
):
    count, halo = lax.axis_size("row"), conv_weight.shape[0]
    keys, values, north, south = gather(fine, parent, w_query, w_key, w_value, count, halo)
    return step(
        fine, north, south, keys, values, coverage, owner_slot, norm_gain, conv_weight, conv_bias
    )


def solution(mesh):
    spread = P(("groups", "row"), None, None)
    placed = (spread, spread, P("groups", None), P("groups")) + (P(),) * 6
    return jax.shard_map(
        on_device, mesh=mesh, in_specs=placed, out_specs=spread, check_vma=False
    )
```

```python
import functools

import jax
import jax.numpy as jnp
from jax import lax
from jax.experimental import pallas as pl
from jax.experimental.pallas import tpu as pltpu
from jax.sharding import PartitionSpec as P

SUB = 16
LOG2E = 1.4426950408889634
VMEM_LIMIT = 56 * 1024 * 1024
MESH = pl.DeviceIdType.MESH


def gather_kernel(
    lines,
    fine_ref,
    parent_ref,
    wq_ref,
    wk_ref,
    wv_ref,
    keys_ref,
    values_ref,
    north_ref,
    south_ref,
    own_k,
    own_v,
    local_sem,
    send_sem,
    recv_sem,
    halo_send,
    halo_recv,
):
    me = lax.axis_index("row")
    count = 4 * lines
    core, col, line = lax.rem(me, 2), lax.rem(lax.div(me, 2), 2), lax.div(me, 4)
    side, halo, chans = fine_ref.shape[0], north_ref.shape[0], wq_ref.shape[0]
    sibling = me + 1 - 2 * core
    across = me + 2 - 4 * col
    ring_next, ring_prev = lax.rem(me + 1, count), lax.rem(me + count - 1, count)
    outer = lax.rem(me + 2 * core - 1 + count, count)
    up = (line < lines - 1, me + 4)
    down = (line > 0, me - 4)

    barrier = pltpu.get_barrier_semaphore()
    for peer in (across, sibling, outer):
        pl.semaphore_signal(barrier, inc=1, device_id={"row": peer}, device_id_type=MESH)
    for exists, peer in (up, down):

        @pl.when(exists)
        def _():
            pl.semaphore_signal(barrier, inc=1, device_id={"row": peer}, device_id_type=MESH)

    parent = parent_ref[0]
    f32 = jnp.float32
    keys = jnp.dot(parent, wk_ref[...], preferred_element_type=f32).astype(jnp.bfloat16)
    keys = lax.dot_general(wq_ref[...], keys, (((1,), (1,)), ((), ())), preferred_element_type=f32)
    own_k[...] = (keys * (LOG2E / chans**0.5)).astype(jnp.bfloat16)
    values = jnp.dot(parent, wv_ref[...], preferred_element_type=f32)
    own_v[...] = values.astype(jnp.bfloat16)
    inside = jnp.minimum(line, 1) + jnp.minimum(lines - 1 - line, 1)
    pl.semaphore_wait(barrier, 3 + inside)

    held = (keys_ref, values_ref)
    owned = (own_k, own_v)

    def copy_of(way, kind, block, turn, peer, own=False):
        return pltpu.make_async_remote_copy(
            src_ref=owned[kind] if own else held[kind].at[block],
            dst_ref=held[kind].at[block],
            send_sem=send_sem.at[way, kind, turn],
            recv_sem=recv_sem.at[kind, block],
            device_id={"row": peer},
            device_id_type=MESH,
        )

    def arrived(kind, block):
        copy_of(3, kind, block, 0, sibling).wait_recv()

    for kind in range(2):
        for way, (exists, peer) in enumerate((up, down)):

            @pl.when(exists)
            def _():
                copy_of(way, kind, me, 0, peer, True).start()

        copy_of(2, kind, me, 0, across, True).start()
    for kind in range(2):
        copy_of(3, kind, me, 0, sibling, True).start()
    local = [pltpu.make_async_copy(owned[k], held[k].at[me], local_sem.at[k]) for k in range(2)]
    edges = [
        pltpu.make_async_remote_copy(
            src_ref=fine_ref.at[pl.ds(first, halo)],
            dst_ref=dst,
            send_sem=halo_send.at[i],
            recv_sem=halo_recv.at[i],
            device_id={"row": peer},
            device_id_type=MESH,
        )
        for i, (first, dst, peer) in enumerate(
            ((side - halo, north_ref, ring_next), (0, south_ref, ring_prev))
        )
    ]
    for copy in local + edges:
        copy.start()

    for t in range(lines):
        for kind in range(2):
            if t:
                for way, (exists, peer) in enumerate((up, down)):
                    block = me - 4 * t if way == 0 else me + 4 * t

                    @pl.when(line >= t if way == 0 else line < lines - t)
                    def _():
                        arrived(kind, block)

                        @pl.when(exists)
                        def _():
                            copy_of(way, kind, block, t, peer).start()

                        copy_of(2, kind, block, 2 * t + way, across).start()
                        copy_of(3, kind, block, 4 * t + way, sibling).start()

        for kind in range(2):
            for way in range(2 if t else 1):
                source = across - 4 * t if way == 0 else across + 4 * t

                @pl.when(line >= t if way == 0 else line < lines - t)
                def _():
                    arrived(kind, source)
                    copy_of(3, kind, source, 4 * t + 2 + way, sibling).start()

    for t in range(lines):
        for way in range(2 if t else 1):
            shift = -4 * t if way == 0 else 4 * t

            @pl.when(line >= t if way == 0 else line < lines - t)
            def _():
                for kind in range(2):
                    arrived(kind, sibling + shift)
                    arrived(kind, sibling + (across - me) + shift)
                    copy_of(2, kind, me, 2 * t + way, across).wait_send()
                    copy_of(3, kind, me, 4 * t + way, sibling).wait_send()
                    copy_of(3, kind, me, 4 * t + 2 + way, sibling).wait_send()

        for way, (exists, peer) in enumerate((up, down)):
            has = line >= t if way == 0 else line < lines - t

            @pl.when(jnp.logical_and(has, exists))
            def _():
                for kind in range(2):
                    copy_of(way, kind, me, t, peer).wait_send()

    for copy in local + edges:
        copy.wait()


def gather(fine, parent, w_query, w_key, w_value, count, halo):
    _, width, chans = fine.shape
    key_rows = parent.shape[1]
    lines = count // 4
    vmem, anywhere = pl.BlockSpec(memory_space=pltpu.VMEM), pl.BlockSpec(memory_space=pl.ANY)
    bf16 = jnp.bfloat16
    edge = jax.ShapeDtypeStruct((halo, width, chans), bf16)
    dma = pltpu.SemaphoreType.DMA
    return pl.pallas_call(
        functools.partial(gather_kernel, lines),
        in_specs=[anywhere] + [vmem] * 4,
        out_specs=[vmem] * 2 + [anywhere] * 2,
        out_shape=[
            jax.ShapeDtypeStruct((count, chans, key_rows), bf16),
            jax.ShapeDtypeStruct((count, key_rows, chans), bf16),
            edge,
            edge,
        ],
        scratch_shapes=[
            pltpu.VMEM((chans, key_rows), bf16),
            pltpu.VMEM((key_rows, chans), bf16),
            dma((2,)),
            dma((4, 2, 4 * lines)),
            dma((2, count)),
            dma((2,)),
            dma((2,)),
        ],
        compiler_params=pltpu.CompilerParams(
            collective_id=0, has_side_effects=True, vmem_limit_bytes=VMEM_LIMIT
        ),
        name="gather",
    )(fine, parent, w_query, w_key, w_value)


def edge_columns(first, last):
    lane = lax.broadcasted_iota(jnp.int32, first.shape, first.ndim - 2)
    axis = first.ndim - 2
    west = jnp.where(lane == 0, 0.0, pltpu.roll(last, 1, axis))
    east = jnp.where(lane == SUB - 1, 0.0, pltpu.roll(first, SUB - 1, axis))
    return west, east


def step_kernel(
    tile_cols,
    cover_ref,
    owner_ref,
    fine_ref,
    north_ref,
    south_ref,
    keys_ref,
    values_ref,
    gain_ref,
    w_ref,
    b_ref,
    out_ref,
    tile_k,
    tile_v,
    scores_a,
    scores_b,
    weights_a,
    weights_b,
    mixed,
    wide,
    state_a,
    state_b,
    flat,
    acc_a,
    acc_b,
    sems,
):
    layers, _, _, chans, _ = w_ref.shape
    side, width, _ = fine_ref.shape
    steps = width // SUB
    halo = north_ref.shape[0]
    position, count = lax.axis_index("row"), keys_ref.shape[0]
    key_rows = values_ref.shape[1]
    span = width // tile_cols
    deep = scores_a.shape[0] // span
    per_tile = side // deep
    chunks = tile_cols * per_tile

    loads = [
        pltpu.make_async_copy(src, mixed.at[pl.ds(at, src.shape[0])], sems.at[i])
        for i, (src, at) in enumerate(
            ((north_ref, 0), (fine_ref, halo), (south_ref, halo + side))
        )
    ]
    for copy in loads:
        copy.start()
    above, below = jnp.maximum(position - 1, 0), jnp.minimum(position + 1, count - 1)
    for k in range(tile_cols):
        for place, tile_row in enumerate((above, position, below)):
            for j in range(cover_ref.shape[1]):
                slot = owner_ref[cover_ref[tile_row * tile_cols + k, j]]
                rows = slice(j * key_rows, (j + 1) * key_rows)
                tile_k[3 * k + place, :, rows] = keys_ref[slot]
                tile_v[3 * k + place, rows, :chans] = values_ref[slot]
                tile_v[3 * k + place, rows, chans:] = jnp.ones((key_rows, chans), jnp.bfloat16)
    for copy in loads:
        copy.wait()

    def place_of(c):
        k, block = lax.div(c, per_tile), lax.rem(c, per_tile)
        cols = pl.ds(pl.multiple_of(k * span, span), span)
        return 3 * k + 1, pl.ds(halo + block * deep, deep), cols

    def score(place, dst):
        tile, rows, cols = place
        mine = mixed[rows, cols]
        mine = mine.reshape(mine.shape[0] * span, chans)
        num = mine.shape[0]
        dst[:num] = jnp.dot(mine, tile_k[tile], preferred_element_type=jnp.float32)

    def soften(src, dst, num):
        for at in range(0, num, 32):
            some = src[at : at + 32]
            top = jnp.max(some, axis=-1, keepdims=True)
            dst[at : at + 32] = jnp.exp2(some - top).astype(jnp.bfloat16)

    def blend(place, weights):
        tile, rows, cols = place
        mine = mixed[rows, cols]
        mine = mine.reshape(mine.shape[0] * span, chans).astype(jnp.float32)
        num = mine.shape[0]
        summed = jnp.dot(weights[:num], tile_v[tile], preferred_element_type=jnp.float32)
        attended = summed[:, :chans] / summed[:, chans:]
        meansq = jnp.mean(attended * attended, axis=-1, keepdims=True)
        new = mine + gain_ref[...] * attended * lax.rsqrt(meansq + 1e-06)
        mixed[rows, cols] = new.astype(jnp.bfloat16).reshape(num // span, span, chans)

    edges = [
        (3 * k + place, slice(at, at + halo), slice(k * span, (k + 1) * span))
        for k in range(tile_cols)
        for place, at in ((0, 0), (2, halo + side))
    ]
    buffers = ((scores_a, weights_a), (scores_b, weights_b))
    for i, place in enumerate(edges):
        scores, weights = buffers[i % 2]
        score(place, scores)
        soften(scores, weights, halo * span)
        blend(place, weights)

    full = deep * span
    score(place_of(0), scores_a)
    score(place_of(1), scores_b)
    soften(scores_a, weights_a, full)

    @pl.loop(1, chunks - 1, step=2)
    def _(c):
        score(place_of(c + 1), scores_a)
        soften(scores_b, weights_b, full)
        blend(place_of(c - 1), weights_a)
        score(place_of(c + 2), scores_b)
        soften(scores_a, weights_a, full)
        blend(place_of(c), weights_b)

    soften(scores_b, weights_b, full)
    blend(place_of(chunks - 2), weights_a)
    blend(place_of(chunks - 1), weights_b)

    at_end = (position == 0, position == count - 1)
    for end, low in ((0, 0), (1, halo + side)):

        @pl.when(at_end[end])
        def _():
            mixed[low : low + halo] = jnp.zeros((halo, width, chans), jnp.bfloat16)

    def put(dst, parity, pair, num, cells):
        west, east = edge_columns(cells[:, 0], cells[:, steps - 1])
        dst[parity, pl.ds(pair, num), 1 : steps + 1] = cells.astype(jnp.bfloat16)
        dst[parity, pl.ds(pair, num), 0] = west.astype(jnp.bfloat16)
        dst[parity, pl.ds(pair, num), steps + 1] = east.astype(jnp.bfloat16)

    def take_rows(src, src_row, pair, num):
        rows = src[pl.ds(src_row, 2 * num)].astype(jnp.float32)
        flat[0 : 2 * num * width] = rows.reshape(2 * num * width, chans)
        for parity in range(2):
            for p in range(num):
                base = (2 * p + parity) * width
                cells = jnp.stack(
                    [flat[pl.ds(base + i, SUB, stride=steps), :] for i in range(steps)]
                )
                put(state_a, parity, pair + p, 1, cells[None])

    @pl.loop(0, (side + 2 * halo) // 8)
    def _(c):
        take_rows(mixed, c * 8, c * 4, 4)

    for layer in range(layers):
        for dx in range(3):
            for r in range(4):
                for o in range(2):
                    dy = r - o
                    at = (dx * 4 + r) * chans
                    if 0 <= dy <= 2:
                        block = w_ref[layer, dy, dx] * jnp.bfloat16(0.5)
                    else:
                        block = jnp.zeros((chans, chans), jnp.bfloat16)
                    wide[layer, at : at + chans, o * chans : (o + 1) * chans] = block

    src, dst = state_a, state_b
    for layer in range(layers):
        pairs = (side + 2 * (halo - 1 - layer)) // 2
        last = layer == layers - 1
        size = min((8, 9), key=lambda n: (-(-pairs // n) * n, -n))
        trips = -(-pairs // size)
        bias = b_ref[layer] * 0.5
        bias = jnp.concatenate([bias, bias])[None, :]

        def first_of(t):
            return jnp.minimum(t * size, pairs - size)

        def multiply(t, acc):
            pair = first_of(t)
            lhs = jnp.concatenate(
                [
                    src[parity, pl.ds(pair + off, size), dx : dx + steps].reshape(
                        size * width, chans
                    )
                    for dx in range(3)
                    for off in range(2)
                    for parity in range(2)
                ],
                axis=1,
            )
            acc[: size * width] = jnp.dot(lhs, wide[layer], preferred_element_type=jnp.float32)

        def activate(t, acc, base):
            pair = first_of(t)
            for p in range(size):
                h = acc[p * width : (p + 1) * width] + bias
                h = h + h * jnp.tanh(h)
                for parity in range(2):
                    cells = h[:, parity * chans : (parity + 1) * chans]
                    cells = cells.reshape(1, steps, SUB, chans)
                    if not last:
                        put(dst, parity, pair + p, 1, cells)
                        continue
                    at = base + (2 * p + parity) * width
                    for i in range(steps):
                        flat[pl.ds(at + i, SUB, stride=steps), :] = cells[0, i]
                    out_ref[2 * (pair + p) + parity] = flat[at : at + width, :].astype(
                        jnp.bfloat16
                    )

        multiply(0, acc_a)

        @pl.loop(0, (trips - 1) // 2)
        def _(t):
            multiply(2 * t + 1, acc_b)
            activate(2 * t, acc_a, 0)
            multiply(2 * t + 2, acc_a)
            activate(2 * t + 1, acc_b, 2 * size * width)

        if trips % 2 == 0:
            multiply(trips - 1, acc_b)
            activate(trips - 2, acc_a, 0)
            activate(trips - 1, acc_b, 2 * size * width)
        else:
            activate(trips - 1, acc_a, 0)

        margin = halo - 1 - layer
        if margin:
            zero_row = jnp.zeros((steps + 2, SUB, chans), jnp.bfloat16)
            for end, low in ((0, 0), (1, 2 * pairs - margin)):

                @pl.when(at_end[end])
                def _():
                    for row in range(low, low + margin):
                        dst[row % 2, row // 2] = zero_row

        src, dst = dst, src


def step(fine, north, south, all_keys, all_values, coverage, owner_slot, gain, weight, bias):
    layers, _, _, chans, _ = weight.shape
    side, width, _ = fine.shape
    halo = north.shape[0]
    tile_cols = width // side
    keys = coverage.shape[1] * all_values.shape[1]
    at_once = side // 4 * side
    bf16, f32 = jnp.bfloat16, jnp.float32
    state = pltpu.VMEM((2, side // 2 + halo, width // SUB + 2, SUB, chans), bf16)
    vmem, smem = pl.BlockSpec(memory_space=pltpu.VMEM), pl.BlockSpec(memory_space=pltpu.SMEM)
    return pl.pallas_call(
        functools.partial(step_kernel, tile_cols),
        in_specs=[smem] * 2 + [pl.BlockSpec(memory_space=pl.ANY)] * 3 + [vmem] * 5,
        out_specs=vmem,
        out_shape=jax.ShapeDtypeStruct(fine.shape, bf16),
        scratch_shapes=[
            pltpu.VMEM((3 * tile_cols, chans, keys), bf16),
            pltpu.VMEM((3 * tile_cols, keys, 2 * chans), bf16),
            pltpu.VMEM((at_once, keys), f32),
            pltpu.VMEM((at_once, keys), f32),
            pltpu.VMEM((at_once, keys), bf16),
            pltpu.VMEM((at_once, keys), bf16),
            pltpu.VMEM((side + 2 * halo, width, chans), bf16),
            pltpu.VMEM((layers, 12 * chans, 2 * chans), bf16),
            state,
            state,
            pltpu.VMEM((36 * width, chans), f32),
            pltpu.VMEM((9 * width, 2 * chans), f32),
            pltpu.VMEM((9 * width, 2 * chans), f32),
            pltpu.SemaphoreType.DMA((3,)),
        ],
        compiler_params=pltpu.CompilerParams(vmem_limit_bytes=VMEM_LIMIT),
        name="step",
    )(
        coverage,
        owner_slot,
        fine,
        north,
        south,
        all_keys,
        all_values,
        gain.reshape(1, chans),
        weight,
        bias,
    )


def on_device(
    fine, parent, coverage, owner_slot, w_query, w_key, w_value, norm_gain, conv_weight, conv_bias
):
    count, halo = lax.axis_size("row"), conv_weight.shape[0]
    keys, values, north, south = gather(fine, parent, w_query, w_key, w_value, count, halo)
    return step(
        fine, north, south, keys, values, coverage, owner_slot, norm_gain, conv_weight, conv_bias
    )


def solution(mesh):
    spread = P(("groups", "row"), None, None)
    placed = (spread, spread, P("groups", None), P("groups")) + (P(),) * 6
    return jax.shard_map(
        on_device, mesh=mesh, in_specs=placed, out_specs=spread, check_vma=False
    )
```
